256 devices in a mesh: dp: 64 (over y, z, core), tensor: 4 (over x).
Axes of the slice: x: 4, y: 4, z: 8, core: 2. Of those that a mesh axis runs over, the one named last changes fastest.
Arguments:
- tokens: bfloat16 [32768, 2560], P('dp', 'tensor'), as said below
- grad_out: bfloat16 [32768, 7168], P('dp', 'tensor'), may hold values from -6 to 6
- error: bfloat16 [64, 2560, 7168], P('dp', None, 'tensor'), may hold values from -120 to 120
- q_start: bfloat16 [7168, 32], P('tensor'), may hold values from -6 to 6
Outputs:
- p_factor: float32 [2560, 32], replicated
- q_factor: float32 [7168, 32], P('tensor')
The draws below stay inside these ranges and needn't reach their ends.
Inputs may be any that keep to these rules, and one draw needn't show every extreme that they name: `tokens`: activations.
All inputs are finite; a program needn't handle non-finite values.
Results may differ from the reference program's by a relative error of at most 0.014.
Values may be sent and summed in bfloat16 or wider, within the bound.
A program may use at most 128 MiB of HBM per device.

```python
import math
import jax
import jax.numpy as jnp
from jax import lax

D = 2560
FF = 7168
R = 32
TOK_DEV = 512
TOKENS = 32768
N_DP = 64


def draw_tokens(key, part):
    key = jax.random.fold_in(key, 11)
    first, second = jax.random.split(key, 2)
    scales = jnp.exp(jax.random.uniform(second, (1, D), jnp.float32, math.log(0.3), math.log(3.0)))
    values = jax.random.normal(first, (TOKENS, D), jnp.float32)
    return (values * scales).astype(jnp.bfloat16)


def level_of(own_key, extent, cuts, low, largest):
    factor_of, own = 1.0, jax.random.fold_in(own_key, 6)
    for axis_at, parts in cuts:
        draws = jnp.exp(jax.random.uniform(jax.random.fold_in(own, axis_at), (parts,), jnp.float32, low / len(cuts), largest / len(cuts)))
        factor_of = factor_of * jnp.repeat(draws, extent[axis_at] // parts).reshape([-1 if axis == axis_at else 1 for axis in range(len(extent))])
    return factor_of


def bell_draw(stream_key, extent, width, reach, cuts=(), kind=jnp.bfloat16):
    values = jax.random.normal(stream_key, extent, jnp.float32) * width
    if len(cuts) > 0:
        values = level_of(stream_key, extent, cuts, -0.22, 0.18) * values
    return jnp.clip(values, min=-reach, max=reach).astype(kind)


def setup_inputs(seed: int = 0) -> dict:
    streams_of = jax.random.split(jax.random.key(seed), 5)
    return {
        "tokens": draw_tokens(jax.random.fold_in(streams_of[4], 71), 0),
        "grad_out": bell_draw(streams_of[1], (TOKENS, FF), 1.0, 6.0, ((0, 64), (1, 4))),
        "error": bell_draw(streams_of[2], (N_DP, D, FF), 20.0, 120.0, ((0, 64), (2, 4))),
        "q_start": bell_draw(streams_of[3], (FF, R), 1.0, 6.0, ((0, 4),)),
    }


def merged_of(tokens, grad_out, error, index):
    start = (index * TOK_DEV).astype(jnp.int32)
    rows = lax.dynamic_slice_in_dim(tokens, start, TOK_DEV, 0)
    outs = lax.dynamic_slice_in_dim(grad_out, start, TOK_DEV, 0)
    grad = lax.dot_general(rows.astype(jnp.float32), outs.astype(jnp.float32), (((0,), (0,)), ((), ())), preferred_element_type=jnp.float32)
    memory = lax.dynamic_index_in_dim(error, index, 0, keepdims=False)
    return grad + memory.astype(jnp.float32)

def reference(tokens, grad_out, error, q_start):
    replicas = jnp.arange(N_DP, dtype=jnp.int32)
    q_wide = q_start.astype(jnp.float32)

    def add_p(total, index):
        merged = merged_of(tokens, grad_out, error, index)
        return (total + jnp.dot(merged, q_wide, precision=lax.Precision.HIGHEST), None)
    p_sum, _ = lax.scan(add_p, jnp.zeros((D, R), jnp.float32), replicas)
    gram = jnp.dot(p_sum.T, p_sum, precision=lax.Precision.HIGHEST)
    lower = jnp.linalg.cholesky(gram)
    p_factor = lax.linalg.triangular_solve(lower, p_sum, left_side=False, lower=True, transpose_a=True) * math.sqrt(D)
    p_wide = p_factor.astype(jnp.bfloat16).astype(jnp.float32)

    def add_q(total, index):
        merged = merged_of(tokens, grad_out, error, index)
        term = lax.dot_general(merged, p_wide, (((0,), (0,)), ((), ())), precision=lax.Precision.HIGHEST)
        return (total + term, None)
    q_total, _ = lax.scan(add_q, jnp.zeros((FF, R), jnp.float32), replicas)
    q_factor = q_total / (N_DP * D)
    return (p_factor, q_factor)
```

```python
import functools
import math

import jax
import jax.numpy as jnp
from jax import lax
from jax.experimental import pallas as pl
from jax.experimental.pallas import tpu as pltpu
from jax.sharding import PartitionSpec as P

MESH = pl.DeviceIdType.MESH
NX, NY, NZ, NC = 4, 4, 8, 2
CHUNKS = 5
BF16, F32 = jnp.bfloat16, jnp.float32
NN = (((1,), (0,)), ((), ()))
NT = (((1,), (1,)), ((), ()))


def mm(a, b, dims, precision=None):
    return lax.dot_general(a, b, dims, precision=precision, preferred_element_type=F32)


def two_part(value):
    high = value.astype(BF16)
    low = (value - high.astype(F32)).astype(BF16)
    return jnp.concatenate([high, low], axis=0)


def folded(value):
    half = value.shape[0] // 2
    return value[:half] + value[half:]


def inverse_factor(gram):
    n = gram.shape[0]
    rows = lax.broadcasted_iota(jnp.int32, (n, n), 0)
    columns = lax.broadcasted_iota(jnp.int32, (n, n), 1)
    unit = (rows == columns).astype(F32)
    both = jnp.concatenate([gram, unit], axis=1)
    at_row = lax.broadcasted_iota(jnp.int32, (n, 1), 0)
    for j in range(n):
        pivot = both[j : j + 1, :]
        scale = both[:, j : j + 1] / pivot[:, j : j + 1]
        both = both - jnp.where(at_row > j, scale, 0.0) * pivot
    diagonal = jnp.sum(jnp.where(rows == columns, both[:, :n], 0.0), axis=1, keepdims=True)
    return both[:, n:] / jnp.sqrt(diagonal)


def kernel(
    tokens_hbm, outs_hbm, error_hbm, q_hbm, p_ref, q_ref,
    tokens, outs, error, q, gq, gq_in, p_mine, p_core, p_xy, p_z, p_all, p_part,
    v, v_in, u, u_core, u_y, u_z, u_all,
    load_sem, gq_sem, core_sem, xy_sem, z_sem, all_sem, sib_sem, v_sem, ucore_sem, uy_sem, uz_sem, uall_sem, usib_sem,
):
    dp, x = lax.axis_index("dp"), lax.axis_index("tensor")
    core, z, y = dp % NC, (dp // NC) % NZ, dp // (NC * NZ)
    width, rank = error.shape[0], q.shape[0]
    half, own_width = rank // 2, tokens.shape[1]
    rows = width // CHUNKS

    def device(dx=0, dy=0, dz=0, dc=0):
        there = ((y + dy) % NY * NZ + (z + dz) % NZ) * NC + (core + dc) % NC
        return (there, (x + dx) % NX)

    sends = []

    def push(src, dst, sems, index, where):
        copy = pltpu.make_async_remote_copy(
            src_ref=src, dst_ref=dst, send_sem=sems.at[0, index], recv_sem=sems.at[1, index],
            device_id=where, device_id_type=MESH,
        )
        copy.start()
        sends.append(copy)
        return copy

    loads = [
        pltpu.make_async_copy(q_hbm, q, load_sem.at[0]),
        pltpu.make_async_copy(outs_hbm, outs, load_sem.at[1]),
    ]
    for k in range(CHUNKS):
        part = pl.ds(k * rows, rows)
        loads.append(pltpu.make_async_copy(error_hbm.at[part], error.at[part], load_sem.at[3 + k]))
    loads.append(pltpu.make_async_copy(tokens_hbm, tokens, load_sem.at[2]))
    for load in loads:
        load.start()

    plane = [(dx, dy) for dx in range(NX) for dy in range(NY) if dx or dy]
    barrier = pltpu.get_barrier_semaphore()
    friends = [device(dx, dy) for dx, dy in plane]
    friends += [device(dz=d) for d in range(1, NZ)] + [device(dc=1)]
    for friend in friends:
        pl.semaphore_signal(barrier, inc=1, device_id=friend, device_id_type=MESH)

    loads[0].wait()
    loads[1].wait()
    gq[...] = mm(q[...], outs[...], NT)
    pl.semaphore_wait(barrier, len(friends))
    gq_copies = [push(gq, gq_in.at[d - 1], gq_sem, d - 1, device(dx=d)) for d in range(1, NX)]

    for k in range(CHUNKS):
        loads[2 + k].wait()
        p_mine[:, k * rows : (k + 1) * rows] = mm(q[...], error[k * rows : (k + 1) * rows, :], NT)

    loads[2 + CHUNKS].wait()
    for copy in gq_copies:
        copy.wait_recv()
    total = gq[...] + gq_in[0] + gq_in[1] + gq_in[2]
    own = pl.ds(pl.multiple_of(x * own_width, 128), own_width)
    p_mine[:, own] = p_mine[:, own] + folded(mm(two_part(total), tokens[...], NN))

    mine, other = pl.ds(core * half, half), pl.ds((1 - core) * half, half)
    push(p_mine.at[other], p_core, core_sem, 0, device(dc=1)).wait_recv()
    p_core[...] = p_core[...] + p_mine[mine, :]

    def piece(dx, dy):
        to = (x + dx) % NX * NY + (y + dy) % NY
        at = pl.multiple_of(5 * (to % 8) // 2 * 128, 128)
        return p_core.at[pl.ds(pl.multiple_of(to // 8 * 8, 8), 8), pl.ds(at, 384)]

    copies = [push(piece(*d), p_xy.at[i], xy_sem, i, device(*d)) for i, d in enumerate(plane)]
    total = piece(0, 0)[...]
    for i, copy in enumerate(copies):
        copy.wait_recv()
        total = total + p_xy[i]

    p_z[z] = total
    copies = [push(p_z.at[z], p_z.at[z], z_sem, d - 1, device(dz=d)) for d in range(1, NZ)]
    for copy in copies:
        copy.wait_recv()
    total = p_z[0]
    for d in range(1, NZ):
        total = total + p_z[d]

    me = x * NY + y
    slot = p_all.at[core, me]
    slot[...] = total
    copies = [push(slot, slot, all_sem, i, device(*d)) for i, d in enumerate(plane)]
    for copy in copies:
        copy.wait_recv()
    push(p_all.at[core], p_all.at[core], sib_sem, 0, device(dc=1)).wait_recv()
    for c in range(NC):
        for r in range(2):
            rank_rows = slice(16 * c + 8 * r, 16 * c + 8 * r + 8)
            for g in range(4):
                p_mine_at = 640 * g
                p_ref[rank_rows, p_mine_at : p_mine_at + 384] = p_all[c, 8 * r + 2 * g]
                p_ref[rank_rows, p_mine_at + 384 : p_mine_at + 640] = p_all[c, 8 * r + 2 * g + 1, :, 128:384]

    p_part[...] = two_part(p_ref[...])
    v[...] = folded(mm(p_part[:, own], tokens[...], NT))
    v_copies = [push(v, v_in.at[d - 1], v_sem, d - 1, device(dx=d)) for d in range(1, NX)]
    from_error = folded(mm(p_part[...], error[...], NN))
    for copy in v_copies:
        copy.wait_recv()
    total = two_part(v[...] + v_in[0] + v_in[1] + v_in[2])
    u[...] = from_error + folded(mm(total, outs[...], NN))

    push(u.at[other], u_core, ucore_sem, 0, device(dc=1)).wait_recv()
    u_core[...] = u_core[...] + u[mine, :]
    long = u_core.shape[1] // 2

    def quarter(dy):
        to = (y + dy) % NY
        at = pl.multiple_of(to % 2 * long, 128)
        return u_core.at[pl.ds(pl.multiple_of(to // 2 * 8, 8), 8), pl.ds(at, long)]

    copies = [push(quarter(d), u_y.at[d - 1], uy_sem, d - 1, device(dy=d)) for d in range(1, NY)]
    total = quarter(0)[...]
    for i, copy in enumerate(copies):
        copy.wait_recv()
        total = total + u_y[i]
    u_z[z] = total
    copies = [push(u_z.at[z], u_z.at[z], uz_sem, d - 1, device(dz=d)) for d in range(1, NZ)]

    p_sum = p_ref[...]
    gram = mm(p_sum, p_sum, NT, lax.Precision.HIGHEST)
    inverse = inverse_factor(gram)
    p_ref[...] = mm(inverse * math.sqrt(width), p_sum, NN, lax.Precision.HIGHEST)

    for copy in copies:
        copy.wait_recv()
    total = u_z[0]
    for d in range(1, NZ):
        total = total + u_z[d]
    slot = u_all.at[core, y]
    slot[...] = total
    copies = [push(slot, slot, uall_sem, d - 1, device(dy=d)) for d in range(1, NY)]
    for copy in copies:
        copy.wait_recv()
    push(u_all.at[core], u_all.at[core], usib_sem, 0, device(dc=1)).wait_recv()
    scaled = inverse * (1.0 / (NC * NZ * NY * math.sqrt(width)))
    for side in range(2):
        total = jnp.concatenate([u_all[0, side], u_all[0, 2 + side], u_all[1, side], u_all[1, 2 + side]], axis=0)
        q_ref[:, side * long : (side + 1) * long] = mm(scaled, total, NN, lax.Precision.HIGHEST)
    for copy in sends:
        copy.wait_send()


def on_device(tokens, grad_out, error, q_start):
    width, hidden = error.shape[1:]
    rank, count, own_width = q_start.shape[1], tokens.shape[0], tokens.shape[1]
    vmem, dma = pltpu.VMEM, pltpu.SemaphoreType.DMA
    p_factor, q_factor = pl.pallas_call(
        kernel,
        out_shape=(
            jax.ShapeDtypeStruct((rank, width), F32),
            jax.ShapeDtypeStruct((rank, hidden), F32),
        ),
        in_specs=[pl.BlockSpec(memory_space=pl.ANY)] * 4,
        out_specs=(pl.BlockSpec(memory_space=pltpu.VMEM),) * 2,
        scratch_shapes=[
            vmem((count, own_width), BF16),
            vmem((count, hidden), BF16),
            vmem((width, hidden), BF16),
            vmem((rank, hidden), BF16),
            vmem((rank, count), F32),
            vmem((NX - 1, rank, count), F32),
            vmem((rank, width), F32),
            vmem((rank // 2, width), F32),
            vmem((NX * NY - 1, 8, 384), F32),
            vmem((NZ, 8, 384), F32),
            vmem((NC, NX * NY, 8, 384), F32),
            vmem((2 * rank, width), BF16),
            vmem((rank, count), F32),
            vmem((NX - 1, rank, count), F32),
            vmem((rank, hidden), F32),
            vmem((rank // 2, hidden), F32),
            vmem((NY - 1, 8, hidden // 2), F32),
            vmem((NZ, 8, hidden // 2), F32),
            vmem((NC, NY, 8, hidden // 2), F32),
            dma((3 + CHUNKS,)),
            dma((2, NX - 1)),
            dma((2, 1)),
            dma((2, NX * NY - 1)),
            dma((2, NZ - 1)),
            dma((2, NX * NY - 1)),
            dma((2, 1)),
            dma((2, NX - 1)),
            dma((2, 1)),
            dma((2, NY - 1)),
            dma((2, NZ - 1)),
            dma((2, NY - 1)),
            dma((2, 1)),
        ],
        compiler_params=pltpu.CompilerParams(
            collective_id=0, has_side_effects=True, vmem_limit_bytes=44 << 20
        ),
    )(tokens, grad_out, error[0], q_start.T)
    return (p_factor.T, q_factor.T)


def solution(mesh):
    in_specs = (P("dp", "tensor"), P("dp", "tensor"), P("dp", None, "tensor"), P("tensor", None))
    out_specs = (P(), P("tensor", None))
    return jax.shard_map(
        on_device, mesh=mesh, in_specs=in_specs, out_specs=out_specs, check_vma=False
    )
```

```python
import functools
import math

import jax
import jax.numpy as jnp
from jax import lax
from jax.experimental import pallas as pl
from jax.experimental.pallas import tpu as pltpu
from jax.sharding import PartitionSpec as P

MESH = pl.DeviceIdType.MESH
NX, NY, NZ, NC = 4, 4, 8, 2
FAR_FIRST, NEAR_FIRST = (2, 1, 3), (1, 3, 2)
BF16, F32 = jnp.bfloat16, jnp.float32
NN = (((1,), (0,)), ((), ()))
NT = (((1,), (1,)), ((), ()))


def mm(a, b, dims, precision=None):
    return lax.dot_general(a, b, dims, precision=precision, preferred_element_type=F32)


def two_part(value):
    high = value.astype(BF16)
    low = (value - high.astype(F32)).astype(BF16)
    return jnp.concatenate([high, low], axis=0)


def folded(value):
    half = value.shape[0] // 2
    return value[:half] + value[half:]


def inverse_factor(gram):
    n = gram.shape[0]
    rows = lax.broadcasted_iota(jnp.int32, (n, n), 0)
    columns = lax.broadcasted_iota(jnp.int32, (n, n), 1)
    unit = (rows == columns).astype(F32)
    both = jnp.concatenate([gram, unit], axis=1)
    at_row = lax.broadcasted_iota(jnp.int32, (n, 1), 0)
    for j in range(n):
        pivot = both[j : j + 1, :]
        scale = both[:, j : j + 1] / pivot[:, j : j + 1]
        both = both - jnp.where(at_row > j, scale, 0.0) * pivot
    diagonal = jnp.sum(jnp.where(rows == columns, both[:, :n], 0.0), axis=1, keepdims=True)
    return both[:, n:] / jnp.sqrt(diagonal)


def kernel(
    tokens_hbm, outs_hbm, error_hbm, q_hbm, p_ref, q_ref,
    tokens, outs, error, q, gq, gq_in, p_mine, p_core, p_xy, own, own_in, p_z, p_all,
    v, v_in, u, u_in, u_z, u_all,
    load_sem, gq_sem, core_sem, xy_sem, own_sem, z_sem, near_sem, all_sem, sib_sem, v_sem, u_sem, uz_sem, uall_sem,
):
    dp, x = lax.axis_index("dp"), lax.axis_index("tensor")
    core, z, y = dp % NC, (dp // NC) % NZ, dp // (NC * NZ)
    block, hidden = error.shape[1:]
    width, rank = NX * block, q.shape[0]
    half, long = rank // 2, hidden // 2

    def device(dx=0, dy=0, dz=0, dc=0):
        there = ((y + dy) % NY * NZ + (z + dz) % NZ) * NC + (core + dc) % NC
        return (there, (x + dx) % NX)

    sends = []

    def push(src, dst, sems, index, where):
        copy = pltpu.make_async_remote_copy(
            src_ref=src, dst_ref=dst, send_sem=sems.at[0, index], recv_sem=sems.at[1, index],
            device_id=where, device_id_type=MESH,
        )
        copy.start()
        sends.append(copy)
        return copy

    def load(src, dst, index):
        copy = pltpu.make_async_copy(src, dst, load_sem.at[index])
        copy.start()
        return copy

    q_load = load(q_hbm, q, 0)
    outs_load = load(outs_hbm, outs, 1)
    error_load = {}
    for dx in FAR_FIRST + (0,):
        at = pl.ds(pl.multiple_of((x + dx) % NX * block, block), block)
        error_load[dx] = load(error_hbm.at[at], error.at[dx], 3 + dx)
    tokens_load = load(tokens_hbm, tokens, 2)

    plane = [(dx, dy) for dx in FAR_FIRST for dy in (2, 1, 3, 0)]
    beside = [(dy, dc) for dy in (2, 1, 3, 0) for dc in range(NC) if dy or dc]
    along = (4, 3, 5, 2, 6, 1, 7)
    barrier = pltpu.get_barrier_semaphore()
    friends = [device(dx, dy) for dx, dy in plane] + [device(dy=dy, dc=dc) for dy, dc in beside]
    friends += [device(dz=d) for d in along]
    for friend in friends:
        pl.semaphore_signal(barrier, inc=1, device_id=friend, device_id_type=MESH)

    q_load.wait()
    outs_load.wait()
    gq[...] = mm(q[...], outs[...], NT)
    pl.semaphore_wait(barrier, len(friends))
    gq_copies = [push(gq, gq_in.at[dx - 1], gq_sem, dx - 1, device(dx)) for dx in FAR_FIRST]

    def piece(ref, yy):
        rows = pl.ds(pl.multiple_of(yy // 2 * 8, 8), 8)
        return ref.at[rows, pl.ds(pl.multiple_of(yy % 2 * 256, 128), 384)]

    def pass_on(copy, dx):
        copy.wait_recv()
        p_core[dx - 1] = p_core[dx - 1] + p_mine[dx - 1, core]
        return [
            push(piece(p_core.at[dx - 1], (y + dy) % NY), p_xy.at[4 * (dx - 1) + dy], xy_sem, 4 * (dx - 1) + dy, device(dx, dy))
            for dy in (2, 1, 3, 0)
        ]

    copies, before = [], None
    for dx in FAR_FIRST:
        error_load[dx].wait()
        product = mm(q[...], error[dx], NT)
        p_mine[dx - 1, 0] = product[:half]
        p_mine[dx - 1, 1] = product[half:]
        copy = push(p_mine.at[dx - 1, 1 - core], p_core.at[dx - 1], core_sem, dx - 1, device(dc=1))
        if before is not None:
            copies += pass_on(*before)
        before = (copy, dx)
    error_load[0].wait()
    product = mm(q[...], error[0], NT)
    copies += pass_on(*before)

    tokens_load.wait()
    for copy in gq_copies:
        copy.wait_recv()
    total = gq[...] + gq_in[0] + gq_in[1] + gq_in[2]
    product = product + folded(mm(two_part(total), tokens[...], NN))
    own[0] = product[:half]
    own[1] = product[half:]
    for dy, dc in beside:
        i = 2 * dy + dc - 1
        there = piece(own.at[(core + dc) % NC], (y + dy) % NY)
        copies.append(push(there, own_in.at[i], own_sem, i, device(dy=dy, dc=dc)))
    total = piece(own.at[core], y)[...]
    for copy in copies:
        copy.wait_recv()
    for i in range(12):
        total = total + p_xy[i]
    for i in range(7):
        total = total + own_in[i]

    p_z[z] = total
    copies = [push(p_z.at[z], p_z.at[z], z_sem, d - 1, device(dz=d)) for d in along]
    for copy in copies:
        copy.wait_recv()
    total = p_z[0]
    for d in range(1, NZ):
        total = total + p_z[d]

    slot = p_all.at[x, core, y]
    slot[...] = total
    near = [push(slot, slot, near_sem, 2 * dy + dc - 1, device(dy=dy, dc=dc)) for dy, dc in beside]
    far = {
        dx: [push(slot, slot, all_sem, 4 * (dx - 1) + dy, device(dx, dy)) for dy in (2, 1, 3, 0)]
        for dx in FAR_FIRST
    }

    def features(at):
        rows = []
        for c in range(NC):
            for r in range(2):
                left, right = p_all[at, c, 2 * r], p_all[at, c, 2 * r + 1]
                rows.append(jnp.concatenate([left, right[:, 128:]], axis=1))
        return jnp.concatenate(rows, axis=0)

    for copy in near:
        copy.wait_recv()
    parts = two_part(features(x))
    v[...] = folded(mm(parts, tokens[...], NT))
    v_copies = [push(v, v_in.at[dx - 1], v_sem, dx - 1, device(dx)) for dx in FAR_FIRST]
    result = folded(mm(parts, error[0], NN))
    forward = {}
    for dx in NEAR_FIRST:
        for copy in far[dx]:
            copy.wait_recv()
        rows = p_all.at[(x + NX - dx) % NX, core]
        forward[dx] = push(rows, rows, sib_sem, dx - 1, device(dc=1))
    for dx in NEAR_FIRST:
        forward[dx].wait_recv()
        parts = two_part(features((x + NX - dx) % NX))
        result = result + folded(mm(parts, error[NX - dx], NN))
    for copy in v_copies:
        copy.wait_recv()
    total = two_part(v[...] + v_in[0] + v_in[1] + v_in[2])
    result = result + folded(mm(total, outs[...], NN))

    u[0] = result[:half]
    u[1] = result[half:]

    def quarter(dy, dc):
        to = (y + dy) % NY
        rows = pl.ds(pl.multiple_of(to // 2 * 8, 8), 8)
        return u.at[(core + dc) % NC, rows, pl.ds(pl.multiple_of(to % 2 * long, 128), long)]

    copies = [
        push(quarter(dy, dc), u_in.at[2 * dy + dc - 1], u_sem, 2 * dy + dc - 1, device(dy=dy, dc=dc))
        for dy, dc in beside
    ]
    total = quarter(0, 0)[...]
    for copy in copies:
        copy.wait_recv()
    for i in range(7):
        total = total + u_in[i]
    u_z[z] = total
    copies = [push(u_z.at[z], u_z.at[z], uz_sem, d - 1, device(dz=d)) for d in along]

    for at in range(NX):
        p_ref[:, at * block : (at + 1) * block] = features(at)
    p_sum = p_ref[...]
    gram = mm(p_sum, p_sum, NT, lax.Precision.HIGHEST)
    inverse = inverse_factor(gram)
    p_ref[...] = mm(inverse * math.sqrt(width), p_sum, NN, lax.Precision.HIGHEST)

    for copy in copies:
        copy.wait_recv()
    total = u_z[0]
    for d in range(1, NZ):
        total = total + u_z[d]
    slot = u_all.at[core, y]
    slot[...] = total
    copies = [push(slot, slot, uall_sem, 2 * dy + dc - 1, device(dy=dy, dc=dc)) for dy, dc in beside]
    for copy in copies:
        copy.wait_recv()
    scaled = inverse * (1.0 / (NC * NZ * NY * math.sqrt(width)))
    for side in range(2):
        total = jnp.concatenate([u_all[0, side], u_all[0, 2 + side], u_all[1, side], u_all[1, 2 + side]], axis=0)
        q_ref[:, side * long : (side + 1) * long] = mm(scaled, total, NN, lax.Precision.HIGHEST)
    for copy in sends:
        copy.wait_send()


def on_device(tokens, grad_out, error, q_start):
    width, hidden = error.shape[1:]
    rank, count, own_width = q_start.shape[1], tokens.shape[0], tokens.shape[1]
    vmem, dma = pltpu.VMEM, pltpu.SemaphoreType.DMA
    p_factor, q_factor = pl.pallas_call(
        kernel,
        out_shape=(
            jax.ShapeDtypeStruct((rank, width), F32),
            jax.ShapeDtypeStruct((rank, hidden), F32),
        ),
        in_specs=[pl.BlockSpec(memory_space=pl.ANY)] * 4,
        out_specs=(pl.BlockSpec(memory_space=pltpu.VMEM),) * 2,
        scratch_shapes=[
            vmem((count, own_width), BF16),
            vmem((count, hidden), BF16),
            vmem((NX, own_width, hidden), BF16),
            vmem((rank, hidden), BF16),
            vmem((rank, count), F32),
            vmem((NX - 1, rank, count), F32),
            vmem((NX - 1, NC, rank // 2, own_width), F32),
            vmem((NX - 1, rank // 2, own_width), F32),
            vmem(((NX - 1) * NY, 8, 384), F32),
            vmem((NC, rank // 2, own_width), F32),
            vmem((NC * NY - 1, 8, 384), F32),
            vmem((NZ, 8, 384), F32),
            vmem((NX, NC, NY, 8, 384), F32),
            vmem((rank, count), F32),
            vmem((NX - 1, rank, count), F32),
            vmem((NC, rank // 2, hidden), F32),
            vmem((NC * NY - 1, 8, hidden // 2), F32),
            vmem((NZ, 8, hidden // 2), F32),
            vmem((NC, NY, 8, hidden // 2), F32),
            dma((3 + NX,)),
            dma((2, NX - 1)),
            dma((2, NX - 1)),
            dma((2, (NX - 1) * NY)),
            dma((2, NC * NY - 1)),
            dma((2, NZ - 1)),
            dma((2, NC * NY - 1)),
            dma((2, (NX - 1) * NY)),
            dma((2, NX - 1)),
            dma((2, NX - 1)),
            dma((2, NC * NY - 1)),
            dma((2, NZ - 1)),
            dma((2, NC * NY - 1)),
        ],
        compiler_params=pltpu.CompilerParams(
            collective_id=0, has_side_effects=True, vmem_limit_bytes=60 << 20
        ),
    )(tokens, grad_out, error[0], q_start.T)
    return (p_factor.T, q_factor.T)


def solution(mesh):
    in_specs = (P("dp", "tensor"), P("dp", "tensor"), P("dp", None, "tensor"), P("tensor", None))
    out_specs = (P(), P("tensor", None))
    return jax.shard_map(
        on_device, mesh=mesh, in_specs=in_specs, out_specs=out_specs, check_vma=False
    )
```

```python
import functools
import math

import jax
import jax.numpy as jnp
from jax import lax
from jax.experimental import pallas as pl
from jax.experimental.pallas import tpu as pltpu
from jax.sharding import PartitionSpec as P

MESH = pl.DeviceIdType.MESH
NX, NY, NZ, NC = 4, 4, 8, 2
FAR_FIRST, NEAR_FIRST = (2, 1, 3), (1, 3, 2)
BF16, F32 = jnp.bfloat16, jnp.float32
NN = (((1,), (0,)), ((), ()))
NT = (((1,), (1,)), ((), ()))


def mm(a, b, dims, precision=None):
    return lax.dot_general(a, b, dims, precision=precision, preferred_element_type=F32)


def two_part(value):
    high = value.astype(BF16)
    low = (value - high.astype(F32)).astype(BF16)
    return jnp.concatenate([high, low], axis=0)


def folded(value):
    half = value.shape[0] // 2
    return value[:half] + value[half:]


def inverse_factor(gram):
    n = gram.shape[0]
    rows = lax.broadcasted_iota(jnp.int32, (n, n), 0)
    columns = lax.broadcasted_iota(jnp.int32, (n, n), 1)
    unit = (rows == columns).astype(F32)
    both = jnp.concatenate([gram, unit], axis=1)
    at_row = lax.broadcasted_iota(jnp.int32, (n, 1), 0)
    for j in range(n):
        pivot = both[j : j + 1, :]
        scale = both[:, j : j + 1] / pivot[:, j : j + 1]
        both = both - jnp.where(at_row > j, scale, 0.0) * pivot
    diagonal = jnp.sum(jnp.where(rows == columns, both[:, :n], 0.0), axis=1, keepdims=True)
    return both[:, n:] / jnp.sqrt(diagonal)


def kernel(
    tokens_hbm, outs_hbm, error_hbm, q_hbm, p_ref, scaled_ref, u_all,
    tokens, outs, error, q, gq, gq_in, p_mine, p_core, p_xy, own, own_in, p_z, p_all,
    v, v_in, u, u_in, u_z,
    load_sem, gq_sem, core_sem, xy_sem, own_sem, z_sem, near_sem, all_sem, sib_sem, v_sem, u_sem, uz_sem, uall_sem,
):
    dp, x = lax.axis_index("dp"), lax.axis_index("tensor")
    core, z, y = dp % NC, (dp // NC) % NZ, dp // (NC * NZ)
    block, hidden = error.shape[1:]
    width, rank = NX * block, q.shape[0]
    half, long = rank // 2, hidden // 2

    def device(dx=0, dy=0, dz=0, dc=0):
        there = ((y + dy) % NY * NZ + (z + dz) % NZ) * NC + (core + dc) % NC
        return (there, (x + dx) % NX)

    sends = []

    def push(src, dst, sems, index, where):
        copy = pltpu.make_async_remote_copy(
            src_ref=src, dst_ref=dst, send_sem=sems.at[0, index], recv_sem=sems.at[1, index],
            device_id=where, device_id_type=MESH,
        )
        copy.start()
        sends.append(copy)
        return copy

    def load(src, dst, index):
        copy = pltpu.make_async_copy(src, dst, load_sem.at[index])
        copy.start()
        return copy

    plane = [(dx, dy) for dx in FAR_FIRST for dy in (2, 1, 3, 0)]
    beside = [(dy, dc) for dy in (2, 1, 3, 0) for dc in range(NC) if dy or dc]
    along = (4, 3, 5, 2, 6, 1, 7)
    barrier = pltpu.get_barrier_semaphore()
    friends = [device(dx, dy) for dx, dy in plane] + [device(dy=dy, dc=dc) for dy, dc in beside]
    friends += [device(dz=d) for d in along]
    for friend in friends:
        pl.semaphore_signal(barrier, inc=1, device_id=friend, device_id_type=MESH)

    q_load = load(q_hbm, q, 0)
    part = outs.shape[0] // 2
    outs_load = [load(outs_hbm.at[pl.ds(h * part, part)], outs.at[pl.ds(h * part, part)], 3 + NX + h) for h in range(2)]
    error_load = {}
    for dx in FAR_FIRST + (0,):
        at = pl.ds(pl.multiple_of((x + dx) % NX * block, block), block)
        error_load[dx] = load(error_hbm.at[at], error.at[dx], 3 + dx)
    tokens_load = load(tokens_hbm, tokens, 2)

    q_load.wait()
    for h in range(2):
        outs_load[h].wait()
        gq[h] = mm(q[...], outs[h * part : (h + 1) * part, :], NT)
    pl.semaphore_wait(barrier, len(friends))
    gq_copies = [
        [push(gq.at[h], gq_in.at[dx - 1, h], gq_sem, 2 * dx - 2 + h, device(dx)) for dx in FAR_FIRST] for h in range(2)
    ]

    def piece(ref, yy):
        rows = pl.ds(pl.multiple_of(yy // 2 * 8, 8), 8)
        return ref.at[rows, pl.ds(pl.multiple_of(yy % 2 * 256, 128), 384)]

    def pass_on(copy, dx):
        copy.wait_recv()
        p_core[dx - 1] = p_core[dx - 1] + p_mine[dx - 1, core]
        return [
            push(piece(p_core.at[dx - 1], (y + dy) % NY), p_xy.at[4 * (dx - 1) + dy], xy_sem, 4 * (dx - 1) + dy, device(dx, dy))
            for dy in (2, 1, 3, 0)
        ]

    copies, before = [], None
    for dx in FAR_FIRST:
        error_load[dx].wait()
        product = mm(q[...], error[dx], NT)
        p_mine[dx - 1, 0] = product[:half]
        p_mine[dx - 1, 1] = product[half:]
        copy = push(p_mine.at[dx - 1, 1 - core], p_core.at[dx - 1], core_sem, dx - 1, device(dc=1))
        if before is not None:
            copies += pass_on(*before)
        before = (copy, dx)
    error_load[0].wait()
    product = mm(q[...], error[0], NT)
    copies += pass_on(*before)

    tokens_load.wait()
    for h, arriving in enumerate(gq_copies):
        for copy in arriving:
            copy.wait_recv()
        total = two_part(gq[h] + gq_in[0, h] + gq_in[1, h] + gq_in[2, h])
        product = product + folded(mm(total, tokens[h * part : (h + 1) * part, :], NN))
    own[0] = product[:half]
    own[1] = product[half:]
    for dy, dc in beside:
        i = 2 * dy + dc - 1
        there = piece(own.at[(core + dc) % NC], (y + dy) % NY)
        copies.append(push(there, own_in.at[i], own_sem, i, device(dy=dy, dc=dc)))
    total = piece(own.at[core], y)[...]
    for copy in copies:
        copy.wait_recv()
    for i in range(12):
        total = total + p_xy[i]
    for i in range(7):
        total = total + own_in[i]

    p_z[z] = total
    copies = [push(p_z.at[z], p_z.at[z], z_sem, d - 1, device(dz=d)) for d in along]
    for copy in copies:
        copy.wait_recv()
    total = p_z[0]
    for d in range(1, NZ):
        total = total + p_z[d]

    slot = p_all.at[x, core, y]
    slot[...] = total
    near = [push(slot, slot, near_sem, 2 * dy + dc - 1, device(dy=dy, dc=dc)) for dy, dc in beside]
    far = {
        dx: [push(slot, slot, all_sem, 4 * (dx - 1) + dy, device(dx, dy)) for dy in (2, 1, 3, 0)]
        for dx in FAR_FIRST
    }

    def features(at):
        rows = []
        for c in range(NC):
            for r in range(2):
                left, right = p_all[at, c, 2 * r], p_all[at, c, 2 * r + 1]
                rows.append(jnp.concatenate([left, right[:, 128:]], axis=1))
        return jnp.concatenate(rows, axis=0)

    for copy in near:
        copy.wait_recv()
    parts = two_part(features(x))
    v_copies = []
    for h in range(2):
        v[h] = folded(mm(parts, tokens[h * part : (h + 1) * part, :], NT))
        v_copies.append([push(v.at[h], v_in.at[dx - 1, h], v_sem, 2 * dx - 2 + h, device(dx)) for dx in FAR_FIRST])
    result = folded(mm(parts, error[0], NN))
    forward = {}
    for dx in NEAR_FIRST:
        for copy in far[dx]:
            copy.wait_recv()
        rows = p_all.at[(x + NX - dx) % NX, core]
        forward[dx] = push(rows, rows, sib_sem, dx - 1, device(dc=1))
    for dx in NEAR_FIRST:
        forward[dx].wait_recv()
        parts = two_part(features((x + NX - dx) % NX))
        result = result + folded(mm(parts, error[NX - dx], NN))
    for h, copies in enumerate(v_copies):
        for copy in copies:
            copy.wait_recv()
        total = two_part(v[h] + v_in[0, h] + v_in[1, h] + v_in[2, h])
        result = result + folded(mm(total, outs[h * part : (h + 1) * part, :], NN))

    u[0] = result[:half]
    u[1] = result[half:]

    def quarter(dy, dc):
        to = (y + dy) % NY
        rows = pl.ds(pl.multiple_of(to // 2 * 8, 8), 8)
        return u.at[(core + dc) % NC, rows, pl.ds(pl.multiple_of(to % 2 * long, 128), long)]

    copies = [
        push(quarter(dy, dc), u_in.at[2 * dy + dc - 1], u_sem, 2 * dy + dc - 1, device(dy=dy, dc=dc))
        for dy, dc in beside
    ]
    total = quarter(0, 0)[...]
    for copy in copies:
        copy.wait_recv()
    for i in range(7):
        total = total + u_in[i]
    u_z[z] = total
    copies = [push(u_z.at[z], u_z.at[z], uz_sem, d - 1, device(dz=d)) for d in along]

    for at in range(NX):
        p_ref[:, at * block : (at + 1) * block] = features(at)
    p_sum = p_ref[...]
    gram = mm(p_sum, p_sum, NT, lax.Precision.HIGHEST)
    inverse = inverse_factor(gram)
    p_ref[...] = mm(inverse * math.sqrt(width), p_sum, NN, lax.Precision.HIGHEST)

    scaled_ref[...] = inverse * (1.0 / (NC * NZ * NY * math.sqrt(width)))
    for copy in copies:
        copy.wait_recv()
    total = u_z[0]
    for d in range(1, NZ):
        total = total + u_z[d]
    slot = u_all.at[core, y]
    slot[...] = total
    copies = [push(slot, slot, uall_sem, 2 * dy + dc - 1, device(dy=dy, dc=dc)) for dy, dc in beside]
    for copy in copies:
        copy.wait_recv()
    for copy in sends:
        copy.wait_send()


def finish(p_ref, scaled_ref, u_all, p_hbm, q_hbm, q, sems):
    p_copy = pltpu.make_async_copy(p_ref, p_hbm, sems.at[0])
    p_copy.start()
    long = u_all.shape[-1]
    copies = []
    for side in range(2):
        total = jnp.concatenate([u_all[0, side], u_all[0, 2 + side], u_all[1, side], u_all[1, 2 + side]], axis=0)
        at = pl.ds(side * long, long)
        q[:, at] = mm(scaled_ref[...], total, NN, lax.Precision.HIGHEST)
        copies.append(pltpu.make_async_copy(q.at[:, at], q_hbm.at[:, at], sems.at[1 + side]))
        copies[-1].start()
    p_copy.wait()
    for copy in copies:
        copy.wait()


def on_device(tokens, grad_out, error, q_start):
    width, hidden = error.shape[1:]
    rank, count, own_width = q_start.shape[1], tokens.shape[0], tokens.shape[1]
    vmem, dma = pltpu.VMEM, pltpu.SemaphoreType.DMA
    p_factor, scaled, total = pl.pallas_call(
        kernel,
        out_shape=(
            jax.ShapeDtypeStruct((rank, width), F32),
            jax.ShapeDtypeStruct((rank, rank), F32),
            jax.ShapeDtypeStruct((NC, NY, 8, hidden // 2), F32),
        ),
        in_specs=[pl.BlockSpec(memory_space=pl.ANY)] * 4,
        out_specs=(pl.BlockSpec(memory_space=pltpu.VMEM),) * 3,
        scratch_shapes=[
            vmem((count, own_width), BF16),
            vmem((count, hidden), BF16),
            vmem((NX, own_width, hidden), BF16),
            vmem((rank, hidden), BF16),
            vmem((2, rank, count // 2), F32),
            vmem((NX - 1, 2, rank, count // 2), F32),
            vmem((NX - 1, NC, rank // 2, own_width), F32),
            vmem((NX - 1, rank // 2, own_width), F32),
            vmem(((NX - 1) * NY, 8, 384), F32),
            vmem((NC, rank // 2, own_width), F32),
            vmem((NC * NY - 1, 8, 384), F32),
            vmem((NZ, 8, 384), F32),
            vmem((NX, NC, NY, 8, 384), F32),
            vmem((2, rank, count // 2), F32),
            vmem((NX - 1, 2, rank, count // 2), F32),
            vmem((NC, rank // 2, hidden), F32),
            vmem((NC * NY - 1, 8, hidden // 2), F32),
            vmem((NZ, 8, hidden // 2), F32),
            dma((5 + NX,)),
            dma((2, 2 * NX - 2)),
            dma((2, NX - 1)),
            dma((2, (NX - 1) * NY)),
            dma((2, NC * NY - 1)),
            dma((2, NZ - 1)),
            dma((2, NC * NY - 1)),
            dma((2, (NX - 1) * NY)),
            dma((2, NX - 1)),
            dma((2, 2 * NX - 2)),
            dma((2, NC * NY - 1)),
            dma((2, NZ - 1)),
            dma((2, NC * NY - 1)),
        ],
        compiler_params=pltpu.CompilerParams(
            collective_id=0, has_side_effects=True, vmem_limit_bytes=53 << 20
        ),
    )(tokens, grad_out, error[0], q_start.T)
    p_factor, q_factor = pl.pallas_call(
        finish,
        out_shape=(
            jax.ShapeDtypeStruct((rank, width), F32),
            jax.ShapeDtypeStruct((rank, hidden), F32),
        ),
        in_specs=[pl.BlockSpec(memory_space=pltpu.VMEM)] * 3,
        out_specs=(pl.BlockSpec(memory_space=pl.ANY),) * 2,
        scratch_shapes=[vmem((rank, hidden), F32), dma((3,))],
        compiler_params=pltpu.CompilerParams(vmem_limit_bytes=53 << 20),
    )(p_factor, scaled, total)
    return (p_factor.T, q_factor.T)


def solution(mesh):
    in_specs = (P("dp", "tensor"), P("dp", "tensor"), P("dp", None, "tensor"), P("tensor", None))
    out_specs = (P(), P("tensor", None))
    return jax.shard_map(
        on_device, mesh=mesh, in_specs=in_specs, out_specs=out_specs, check_vma=False
    )
```

```python
import functools
import math

import jax
import jax.numpy as jnp
from jax import lax
from jax.experimental import pallas as pl
from jax.experimental.pallas import tpu as pltpu
from jax.sharding import PartitionSpec as P

MESH = pl.DeviceIdType.MESH
NX, NY, NZ, NC = 4, 4, 8, 2
FAR_FIRST, NEAR_FIRST = (2, 1, 3), (1, 3, 2)
BF16, F32 = jnp.bfloat16, jnp.float32
NN = (((1,), (0,)), ((), ()))
NT = (((1,), (1,)), ((), ()))


def mm(a, b, dims, precision=None):
    return lax.dot_general(a, b, dims, precision=precision, preferred_element_type=F32)


def two_part(value):
    high = value.astype(BF16)
    low = (value - high.astype(F32)).astype(BF16)
    return jnp.concatenate([high, low], axis=0)


def folded(value):
    half = value.shape[0] // 2
    return value[:half] + value[half:]


def inverse_factor(gram):
    n = gram.shape[0]
    rows = lax.broadcasted_iota(jnp.int32, (n, n), 0)
    columns = lax.broadcasted_iota(jnp.int32, (n, n), 1)
    unit = (rows == columns).astype(F32)
    both = jnp.concatenate([gram, unit], axis=1)
    at_row = lax.broadcasted_iota(jnp.int32, (n, 1), 0)
    for j in range(n):
        pivot = both[j : j + 1, :]
        scale = both[:, j : j + 1] / pivot[:, j : j + 1]
        both = both - jnp.where(at_row > j, scale, 0.0) * pivot
    diagonal = jnp.sum(jnp.where(rows == columns, both[:, :n], 0.0), axis=1, keepdims=True)
    return both[:, n:] / jnp.sqrt(diagonal)


def kernel(
    tokens_hbm, outs_hbm, error_hbm, q_hbm, p_ref, scaled_ref, u_all,
    tokens, outs, error, q, gq, gq_in, p_mine, p_core, p_xy, own, own_in, p_z, p_all,
    v, v_in, u, u_in, u_z,
    load_sem, gq_sem, core_sem, xy_sem, own_sem, z_sem, near_sem, all_sem, sib_sem, v_sem, u_sem, uz_sem, uall_sem,
):
    dp, x = lax.axis_index("dp"), lax.axis_index("tensor")
    core, z, y = dp % NC, (dp // NC) % NZ, dp // (NC * NZ)
    block, hidden = error.shape[1:]
    width, rank = NX * block, q.shape[0]
    half, long = rank // 2, hidden // 2

    def device(dx=0, dy=0, dz=0, dc=0):
        there = ((y + dy) % NY * NZ + (z + dz) % NZ) * NC + (core + dc) % NC
        return (there, (x + dx) % NX)

    sends = []

    def push(src, dst, sems, index, where):
        copy = pltpu.make_async_remote_copy(
            src_ref=src, dst_ref=dst, send_sem=sems.at[0, index], recv_sem=sems.at[1, index],
            device_id=where, device_id_type=MESH,
        )
        copy.start()
        sends.append(copy)
        return copy

    def load(src, dst, index):
        copy = pltpu.make_async_copy(src, dst, load_sem.at[index])
        copy.start()
        return copy

    plane = [(dx, dy) for dx in FAR_FIRST for dy in (2, 1, 3, 0)]
    beside = [(dy, dc) for dy in (2, 1, 3, 0) for dc in range(NC) if dy or dc]
    along = (4, 3, 5, 2, 6, 1, 7)
    barrier = pltpu.get_barrier_semaphore()
    friends = [device(*plane[0]), device(dz=along[0])] + [device(dz=d) for d in along[1:3]]
    friends += [device(dx, dy) for dx, dy in plane[1:]] + [device(dz=d) for d in along[3:]]
    friends += [device(dy=dy, dc=dc) for dy, dc in beside]
    for friend in friends:
        pl.semaphore_signal(barrier, inc=1, device_id=friend, device_id_type=MESH)

    q_load = load(q_hbm, q, 0)
    part = outs.shape[0] // 2
    outs_load = [load(outs_hbm.at[pl.ds(h * part, part)], outs.at[pl.ds(h * part, part)], 3 + NX + h) for h in range(2)]
    error_load = {}
    for dx in FAR_FIRST + (0,):
        at = pl.ds(pl.multiple_of((x + dx) % NX * block, block), block)
        error_load[dx] = load(error_hbm.at[at], error.at[dx], 3 + dx)
    tokens_load = load(tokens_hbm, tokens, 2)

    q_load.wait()
    for h in range(2):
        outs_load[h].wait()
        gq[h] = mm(q[...], outs[h * part : (h + 1) * part, :], NT)
    pl.semaphore_wait(barrier, len(friends))
    gq_copies = [
        [push(gq.at[h], gq_in.at[dx - 1, h], gq_sem, 2 * dx - 2 + h, device(dx)) for dx in FAR_FIRST] for h in range(2)
    ]

    def piece(ref, yy):
        rows = pl.ds(pl.multiple_of(yy // 2 * 8, 8), 8)
        return ref.at[rows, pl.ds(pl.multiple_of(yy % 2 * 256, 128), 384)]

    def pass_on(copy, dx):
        copy.wait_recv()
        p_core[dx - 1] = p_core[dx - 1] + p_mine[dx - 1, core]
        return [
            push(piece(p_core.at[dx - 1], (y + dy) % NY), p_xy.at[4 * (dx - 1) + dy], xy_sem, 4 * (dx - 1) + dy, device(dx, dy))
            for dy in (2, 1, 3, 0)
        ]

    copies, before = [], None
    for dx in FAR_FIRST:
        error_load[dx].wait()
        product = mm(q[...], error[dx], NT)
        p_mine[dx - 1, 0] = product[:half]
        p_mine[dx - 1, 1] = product[half:]
        copy = push(p_mine.at[dx - 1, 1 - core], p_core.at[dx - 1], core_sem, dx - 1, device(dc=1))
        if before is not None:
            copies += pass_on(*before)
        before = (copy, dx)
    error_load[0].wait()
    product = mm(q[...], error[0], NT)
    copies += pass_on(*before)

    tokens_load.wait()
    for h, arriving in enumerate(gq_copies):
        for copy in arriving:
            copy.wait_recv()
        total = two_part(gq[h] + gq_in[0, h] + gq_in[1, h] + gq_in[2, h])
        product = product + folded(mm(total, tokens[h * part : (h + 1) * part, :], NN))
    own[0] = product[:half]
    own[1] = product[half:]
    for dy, dc in beside:
        i = 2 * dy + dc - 1
        there = piece(own.at[(core + dc) % NC], (y + dy) % NY)
        copies.append(push(there, own_in.at[i], own_sem, i, device(dy=dy, dc=dc)))
    total = piece(own.at[core], y)[...]
    for copy in copies:
        copy.wait_recv()
    for i in range(12):
        total = total + p_xy[i]
    for i in range(7):
        total = total + own_in[i]

    p_z[z] = total
    copies = [push(p_z.at[z], p_z.at[z], z_sem, d - 1, device(dz=d)) for d in along]
    for copy in copies:
        copy.wait_recv()
    total = p_z[0]
    for d in range(1, NZ):
        total = total + p_z[d]

    slot = p_all.at[x, core, y]
    slot[...] = total
    near = [push(slot, slot, near_sem, 2 * dy + dc - 1, device(dy=dy, dc=dc)) for dy, dc in beside]
    far = {
        dx: [push(slot, slot, all_sem, 4 * (dx - 1) + dy, device(dx, dy)) for dy in (2, 1, 3, 0)]
        for dx in FAR_FIRST
    }

    def features(at):
        rows = []
        for c in range(NC):
            for r in range(2):
                left, right = p_all[at, c, 2 * r], p_all[at, c, 2 * r + 1]
                rows.append(jnp.concatenate([left, right[:, 128:]], axis=1))
        return jnp.concatenate(rows, axis=0)

    for copy in near:
        copy.wait_recv()
    parts = two_part(features(x))
    v_copies = []
    for h in range(2):
        v[h] = folded(mm(parts, tokens[h * part : (h + 1) * part, :], NT))
        v_copies.append([push(v.at[h], v_in.at[dx - 1, h], v_sem, 2 * dx - 2 + h, device(dx)) for dx in FAR_FIRST])
    result = folded(mm(parts, error[0], NN))
    forward = {}
    for dx in NEAR_FIRST:
        for copy in far[dx]:
            copy.wait_recv()
        rows = p_all.at[(x + NX - dx) % NX, core]
        forward[dx] = push(rows, rows, sib_sem, dx - 1, device(dc=1))
    for dx in NEAR_FIRST:
        forward[dx].wait_recv()
        parts = two_part(features((x + NX - dx) % NX))
        result = result + folded(mm(parts, error[NX - dx], NN))
    for h, copies in enumerate(v_copies):
        for copy in copies:
            copy.wait_recv()
        total = two_part(v[h] + v_in[0, h] + v_in[1, h] + v_in[2, h])
        result = result + folded(mm(total, outs[h * part : (h + 1) * part, :], NN))

    u[0] = result[:half]
    u[1] = result[half:]

    def quarter(dy, dc):
        to = (y + dy) % NY
        rows = pl.ds(pl.multiple_of(to // 2 * 8, 8), 8)
        return u.at[(core + dc) % NC, rows, pl.ds(pl.multiple_of(to % 2 * long, 128), long)]

    copies = [
        push(quarter(dy, dc), u_in.at[2 * dy + dc - 1], u_sem, 2 * dy + dc - 1, device(dy=dy, dc=dc))
        for dy, dc in beside
    ]
    total = quarter(0, 0)[...]
    for copy in copies:
        copy.wait_recv()
    for i in range(7):
        total = total + u_in[i]
    u_z[z] = total
    copies = [push(u_z.at[z], u_z.at[z], uz_sem, d - 1, device(dz=d)) for d in along]

    for at in range(NX):
        p_ref[:, at * block : (at + 1) * block] = features(at)
    p_sum = p_ref[...]
    gram = mm(p_sum, p_sum, NT, lax.Precision.HIGHEST)
    inverse = inverse_factor(gram)
    p_ref[...] = mm(inverse * math.sqrt(width), p_sum, NN, lax.Precision.HIGHEST)

    scaled_ref[...] = inverse * (1.0 / (NC * NZ * NY * math.sqrt(width)))
    for copy in copies:
        copy.wait_recv()
    total = u_z[0]
    for d in range(1, NZ):
        total = total + u_z[d]
    slot = u_all.at[core, y]
    slot[...] = total
    copies = [push(slot, slot, uall_sem, 2 * dy + dc - 1, device(dy=dy, dc=dc)) for dy, dc in beside]
    for copy in copies:
        copy.wait_recv()
    for copy in sends:
        copy.wait_send()


def finish(p_ref, scaled_ref, u_all, p_hbm, q_hbm, q, sems):
    p_copy = pltpu.make_async_copy(p_ref, p_hbm, sems.at[0])
    p_copy.start()
    long = u_all.shape[-1]
    copies = []
    for side in range(2):
        total = jnp.concatenate([u_all[0, side], u_all[0, 2 + side], u_all[1, side], u_all[1, 2 + side]], axis=0)
        at = pl.ds(side * long, long)
        q[:, at] = mm(scaled_ref[...], total, NN, lax.Precision.HIGHEST)
        copies.append(pltpu.make_async_copy(q.at[:, at], q_hbm.at[:, at], sems.at[1 + side]))
        copies[-1].start()
    p_copy.wait()
    for copy in copies:
        copy.wait()


def on_device(tokens, grad_out, error, q_start):
    width, hidden = error.shape[1:]
    rank, count, own_width = q_start.shape[1], tokens.shape[0], tokens.shape[1]
    vmem, dma = pltpu.VMEM, pltpu.SemaphoreType.DMA
    p_factor, scaled, total = pl.pallas_call(
        kernel,
        out_shape=(
            jax.ShapeDtypeStruct((rank, width), F32),
            jax.ShapeDtypeStruct((rank, rank), F32),
            jax.ShapeDtypeStruct((NC, NY, 8, hidden // 2), F32),
        ),
        in_specs=[pl.BlockSpec(memory_space=pl.ANY)] * 4,
        out_specs=(pl.BlockSpec(memory_space=pltpu.VMEM),) * 3,
        scratch_shapes=[
            vmem((count, own_width), BF16),
            vmem((count, hidden), BF16),
            vmem((NX, own_width, hidden), BF16),
            vmem((rank, hidden), BF16),
            vmem((2, rank, count // 2), F32),
            vmem((NX - 1, 2, rank, count // 2), F32),
            vmem((NX - 1, NC, rank // 2, own_width), F32),
            vmem((NX - 1, rank // 2, own_width), F32),
            vmem(((NX - 1) * NY, 8, 384), F32),
            vmem((NC, rank // 2, own_width), F32),
            vmem((NC * NY - 1, 8, 384), F32),
            vmem((NZ, 8, 384), F32),
            vmem((NX, NC, NY, 8, 384), F32),
            vmem((2, rank, count // 2), F32),
            vmem((NX - 1, 2, rank, count // 2), F32),
            vmem((NC, rank // 2, hidden), F32),
            vmem((NC * NY - 1, 8, hidden // 2), F32),
            vmem((NZ, 8, hidden // 2), F32),
            dma((5 + NX,)),
            dma((2, 2 * NX - 2)),
            dma((2, NX - 1)),
            dma((2, (NX - 1) * NY)),
            dma((2, NC * NY - 1)),
            dma((2, NZ - 1)),
            dma((2, NC * NY - 1)),
            dma((2, (NX - 1) * NY)),
            dma((2, NX - 1)),
            dma((2, 2 * NX - 2)),
            dma((2, NC * NY - 1)),
            dma((2, NZ - 1)),
            dma((2, NC * NY - 1)),
        ],
        compiler_params=pltpu.CompilerParams(
            collective_id=0, has_side_effects=True, vmem_limit_bytes=53 << 20
        ),
    )(*(pltpu.with_memory_space_constraint(a, pltpu.HBM) for a in (tokens, grad_out, error[0], q_start.T)))
    p_factor, q_factor = pl.pallas_call(
        finish,
        out_shape=(
            jax.ShapeDtypeStruct((rank, width), F32),
            jax.ShapeDtypeStruct((rank, hidden), F32),
        ),
        in_specs=[pl.BlockSpec(memory_space=pltpu.VMEM)] * 3,
        out_specs=(pl.BlockSpec(memory_space=pl.ANY),) * 2,
        scratch_shapes=[vmem((rank, hidden), F32), dma((3,))],
        compiler_params=pltpu.CompilerParams(vmem_limit_bytes=53 << 20),
    )(p_factor, scaled, total)
    return (p_factor.T, q_factor.T)


def solution(mesh):
    in_specs = (P("dp", "tensor"), P("dp", "tensor"), P("dp", None, "tensor"), P("tensor", None))
    out_specs = (P(), P("tensor", None))
    return jax.shard_map(
        on_device, mesh=mesh, in_specs=in_specs, out_specs=out_specs, check_vma=False
    )
```

```python
import functools
import math

import jax
import jax.numpy as jnp
from jax import lax
from jax.experimental import pallas as pl
from jax.experimental.pallas import tpu as pltpu
from jax.sharding import PartitionSpec as P

MESH = pl.DeviceIdType.MESH
NX, NY, NZ, NC = 4, 4, 8, 2
FAR_FIRST, NEAR_FIRST = (2, 1, 3), (1, 3, 2)
BF16, F32 = jnp.bfloat16, jnp.float32
NN = (((1,), (0,)), ((), ()))
NT = (((1,), (1,)), ((), ()))


def mm(a, b, dims, precision=None):
    return lax.dot_general(a, b, dims, precision=precision, preferred_element_type=F32)


def two_part(value):
    high = value.astype(BF16)
    low = (value - high.astype(F32)).astype(BF16)
    return jnp.concatenate([high, low], axis=0)


def folded(value):
    half = value.shape[0] // 2
    return value[:half] + value[half:]


def inverse_factor(gram):
    n = gram.shape[0]
    rows = lax.broadcasted_iota(jnp.int32, (n, n), 0)
    columns = lax.broadcasted_iota(jnp.int32, (n, n), 1)
    unit = (rows == columns).astype(F32)
    both = jnp.concatenate([gram, unit], axis=1)
    at_row = lax.broadcasted_iota(jnp.int32, (n, 1), 0)
    for j in range(n):
        pivot = both[j : j + 1, :]
        scale = both[:, j : j + 1] / pivot[:, j : j + 1]
        both = both - jnp.where(at_row > j, scale, 0.0) * pivot
    diagonal = jnp.sum(jnp.where(rows == columns, both[:, :n], 0.0), axis=1, keepdims=True)
    return both[:, n:] / jnp.sqrt(diagonal)


def kernel(
    tokens_hbm, outs_hbm, error_hbm, q_hbm, p_ref, scaled_ref, u_all,
    tokens, outs, error, q, gq, gq_in, p_mine, p_core, p_xy, own, own_in, p_z, p_all,
    v, v_in, u, u_in, u_z,
    load_sem, gq_sem, core_sem, xy_sem, own_sem, z_sem, near_sem, all_sem, sib_sem, v_sem, u_sem, uz_sem, uall_sem,
):
    dp, x = lax.axis_index("dp"), lax.axis_index("tensor")
    core, z, y = dp % NC, (dp // NC) % NZ, dp // (NC * NZ)
    block, hidden = error.shape[1:]
    width, rank = NX * block, q.shape[0]
    half, long = rank // 2, hidden // 2

    def device(dx=0, dy=0, dz=0, dc=0):
        there = ((y + dy) % NY * NZ + (z + dz) % NZ) * NC + (core + dc) % NC
        return (there, (x + dx) % NX)

    sends = []

    def push(src, dst, sems, index, where):
        copy = pltpu.make_async_remote_copy(
            src_ref=src, dst_ref=dst, send_sem=sems.at[0, index], recv_sem=sems.at[1, index],
            device_id=where, device_id_type=MESH,
        )
        copy.start()
        sends.append(copy)
        return copy

    def load(src, dst, index):
        copy = pltpu.make_async_copy(src, dst, load_sem.at[index])
        copy.start()
        return copy

    plane = [(dx, dy) for dx in FAR_FIRST for dy in (2, 1, 3, 0)]
    beside = [(dy, dc) for dy in (2, 1, 3, 0) for dc in range(NC) if dy or dc]
    along = (4, 3, 5, 2, 6, 1, 7)
    barrier = pltpu.get_barrier_semaphore()
    friends = [device(*plane[0]), device(dz=along[0])] + [device(dz=d) for d in along[1:3]]
    friends += [device(dx, dy) for dx, dy in plane[1:]] + [device(dz=d) for d in along[3:]]
    friends += [device(dy=dy, dc=dc) for dy, dc in beside]
    for friend in friends:
        pl.semaphore_signal(barrier, inc=1, device_id=friend, device_id_type=MESH)

    q_load = load(q_hbm, q, 0)
    part = outs.shape[0] // 2
    outs_load = [load(outs_hbm.at[pl.ds(h * part, part)], outs.at[pl.ds(h * part, part)], 3 + NX + h) for h in range(2)]
    error_load = {}
    for dx in FAR_FIRST + (0,):
        at = pl.ds(pl.multiple_of((x + dx) % NX * block, block), block)
        error_load[dx] = load(error_hbm.at[at], error.at[dx], 3 + dx)
    tokens_load = load(tokens_hbm, tokens, 2)

    q_load.wait()
    for h in range(2):
        outs_load[h].wait()
        gq[h] = mm(q[...], outs[h * part : (h + 1) * part, :], NT)
    pl.semaphore_wait(barrier, len(friends))
    gq_copies = [
        [push(gq.at[h], gq_in.at[dx - 1, h], gq_sem, 2 * dx - 2 + h, device(dx)) for dx in FAR_FIRST] for h in range(2)
    ]

    def piece(ref, yy):
        rows = pl.ds(pl.multiple_of(yy // 2 * 8, 8), 8)
        return ref.at[rows, pl.ds(pl.multiple_of(yy % 2 * 256, 128), 384)]

    def pass_on(copy, dx):
        copy.wait_recv()
        p_core[dx - 1] = p_core[dx - 1] + p_mine[dx - 1, core]
        return [
            push(piece(p_core.at[dx - 1], (y + dy) % NY), p_xy.at[4 * (dx - 1) + dy], xy_sem, 4 * (dx - 1) + dy, device(dx, dy))
            for dy in (2, 1, 3, 0)
        ]

    copies, before = [], None
    for dx in FAR_FIRST:
        error_load[dx].wait()
        product = mm(q[...], error[dx], NT)
        p_mine[dx - 1, 0] = product[:half]
        p_mine[dx - 1, 1] = product[half:]
        copy = push(p_mine.at[dx - 1, 1 - core], p_core.at[dx - 1], core_sem, dx - 1, device(dc=1))
        if before is not None:
            copies += pass_on(*before)
        before = (copy, dx)
    error_load[0].wait()
    product = mm(q[...], error[0], NT)
    copies += pass_on(*before)

    tokens_load.wait()
    for h, arriving in enumerate(gq_copies):
        for copy in arriving:
            copy.wait_recv()
        total = two_part(gq[h] + gq_in[0, h] + gq_in[1, h] + gq_in[2, h])
        product = product + folded(mm(total, tokens[h * part : (h + 1) * part, :], NN))
    own[0] = product[:half]
    own[1] = product[half:]
    for dy, dc in beside:
        i = 2 * dy + dc - 1
        there = piece(own.at[(core + dc) % NC], (y + dy) % NY)
        copies.append(push(there, own_in.at[i], own_sem, i, device(dy=dy, dc=dc)))
    total = piece(own.at[core], y)[...]
    for copy in copies:
        copy.wait_recv()
    for i in range(12):
        total = total + p_xy[i]
    for i in range(7):
        total = total + own_in[i]

    p_z[z] = total
    copies = [push(p_z.at[z], p_z.at[z], z_sem, d - 1, device(dz=d)) for d in along]
    for copy in copies:
        copy.wait_recv()
    total = p_z[0]
    for d in range(1, NZ):
        total = total + p_z[d]

    slot = p_all.at[x, core, y]
    slot[...] = total
    near = [push(slot, slot, near_sem, 2 * dy + dc - 1, device(dy=dy, dc=dc)) for dy, dc in beside]
    far = {
        dx: [push(slot, slot, all_sem, 4 * (dx - 1) + dy, device(dx, dy)) for dy in (2, 1, 3, 0)]
        for dx in FAR_FIRST
    }

    def features(at):
        rows = []
        for c in range(NC):
            for r in range(2):
                left, right = p_all[at, c, 2 * r], p_all[at, c, 2 * r + 1]
                rows.append(jnp.concatenate([left, right[:, 128:]], axis=1))
        return jnp.concatenate(rows, axis=0)

    for copy in near:
        copy.wait_recv()
    parts = two_part(features(x))
    v_copies = []
    for h in range(2):
        v[h] = folded(mm(parts, tokens[h * part : (h + 1) * part, :], NT))
        v_copies.append([push(v.at[h], v_in.at[dx - 1, h], v_sem, 2 * dx - 2 + h, device(dx)) for dx in FAR_FIRST])
    result = folded(mm(parts, error[0], NN))
    forward = {}
    for dx in NEAR_FIRST:
        for copy in far[dx]:
            copy.wait_recv()
        rows = p_all.at[(x + NX - dx) % NX, core]
        forward[dx] = push(rows, rows, sib_sem, dx - 1, device(dc=1))
    for dx in NEAR_FIRST:
        forward[dx].wait_recv()
        parts = two_part(features((x + NX - dx) % NX))
        result = result + folded(mm(parts, error[NX - dx], NN))
    for h, copies in enumerate(v_copies):
        for copy in copies:
            copy.wait_recv()
        total = two_part(v[h] + v_in[0, h] + v_in[1, h] + v_in[2, h])
        result = result + folded(mm(total, outs[h * part : (h + 1) * part, :], NN))

    u[0] = result[:half]
    u[1] = result[half:]

    spans = [pl.ds(0, 512), pl.ds(512, long - 512)]

    def quarter(dy, dc, k):
        to = (y + dy) % NY
        rows = pl.ds(pl.multiple_of(to // 2 * 8, 8), 8)
        at = pl.multiple_of(to % 2 * long + spans[k].start, 128)
        return u.at[(core + dc) % NC, rows, pl.ds(at, spans[k].size)]

    copies = [
        [
            push(quarter(dy, dc, k), u_in.at[2 * dy + dc - 1, :, span], u_sem, 7 * k + 2 * dy + dc - 1, device(dy=dy, dc=dc))
            for dy, dc in beside
        ]
        for k, span in enumerate(spans)
    ]
    z_copies = []
    for k, span in enumerate(spans):
        total = quarter(0, 0, k)[...]
        for copy in copies[k]:
            copy.wait_recv()
        for i in range(7):
            total = total + u_in[i, :, span]
        u_z[z, :, span] = total
        slot = u_z.at[z, :, span]
        z_copies.append([push(slot, slot, uz_sem, 7 * k + d - 1, device(dz=d)) for d in along])

    for at in range(NX):
        p_ref[:, at * block : (at + 1) * block] = features(at)
    p_sum = p_ref[...]
    gram = mm(p_sum, p_sum, NT, lax.Precision.HIGHEST)
    inverse = inverse_factor(gram)
    p_ref[...] = mm(inverse * math.sqrt(width), p_sum, NN, lax.Precision.HIGHEST)

    scaled_ref[...] = inverse * (1.0 / (NC * NZ * NY * math.sqrt(width)))
    copies = []
    for k, span in enumerate(spans):
        for copy in z_copies[k]:
            copy.wait_recv()
        total = u_z[0, :, span]
        for d in range(1, NZ):
            total = total + u_z[d, :, span]
        u_all[core, y, :, span] = total
        slot = u_all.at[core, y, :, span]
        copies += [push(slot, slot, uall_sem, 7 * k + 2 * dy + dc - 1, device(dy=dy, dc=dc)) for dy, dc in beside]
    for copy in copies:
        copy.wait_recv()
    for copy in sends:
        copy.wait_send()


def finish(p_ref, scaled_ref, u_all, p_hbm, q_hbm, q, sems):
    p_copy = pltpu.make_async_copy(p_ref, p_hbm, sems.at[0])
    p_copy.start()
    long = u_all.shape[-1]
    copies = []
    for side in range(2):
        total = jnp.concatenate([u_all[0, side], u_all[0, 2 + side], u_all[1, side], u_all[1, 2 + side]], axis=0)
        at = pl.ds(side * long, long)
        q[:, at] = mm(scaled_ref[...], total, NN, lax.Precision.HIGHEST)
        copies.append(pltpu.make_async_copy(q.at[:, at], q_hbm.at[:, at], sems.at[1 + side]))
        copies[-1].start()
    p_copy.wait()
    for copy in copies:
        copy.wait()


def on_device(tokens, grad_out, error, q_start):
    width, hidden = error.shape[1:]
    rank, count, own_width = q_start.shape[1], tokens.shape[0], tokens.shape[1]
    vmem, dma = pltpu.VMEM, pltpu.SemaphoreType.DMA
    p_factor, scaled, total = pl.pallas_call(
        kernel,
        out_shape=(
            jax.ShapeDtypeStruct((rank, width), F32),
            jax.ShapeDtypeStruct((rank, rank), F32),
            jax.ShapeDtypeStruct((NC, NY, 8, hidden // 2), F32),
        ),
        in_specs=[pl.BlockSpec(memory_space=pl.ANY)] * 4,
        out_specs=(pl.BlockSpec(memory_space=pltpu.VMEM),) * 3,
        scratch_shapes=[
            vmem((count, own_width), BF16),
            vmem((count, hidden), BF16),
            vmem((NX, own_width, hidden), BF16),
            vmem((rank, hidden), BF16),
            vmem((2, rank, count // 2), F32),
            vmem((NX - 1, 2, rank, count // 2), F32),
            vmem((NX - 1, NC, rank // 2, own_width), F32),
            vmem((NX - 1, rank // 2, own_width), F32),
            vmem(((NX - 1) * NY, 8, 384), F32),
            vmem((NC, rank // 2, own_width), F32),
            vmem((NC * NY - 1, 8, 384), F32),
            vmem((NZ, 8, 384), F32),
            vmem((NX, NC, NY, 8, 384), F32),
            vmem((2, rank, count // 2), F32),
            vmem((NX - 1, 2, rank, count // 2), F32),
            vmem((NC, rank // 2, hidden), F32),
            vmem((NC * NY - 1, 8, hidden // 2), F32),
            vmem((NZ, 8, hidden // 2), F32),
            dma((5 + NX,)),
            dma((2, 2 * NX - 2)),
            dma((2, NX - 1)),
            dma((2, (NX - 1) * NY)),
            dma((2, NC * NY - 1)),
            dma((2, NZ - 1)),
            dma((2, NC * NY - 1)),
            dma((2, (NX - 1) * NY)),
            dma((2, NX - 1)),
            dma((2, 2 * NX - 2)),
            dma((2, 14)),
            dma((2, 14)),
            dma((2, 14)),
        ],
        compiler_params=pltpu.CompilerParams(
            collective_id=0, has_side_effects=True, vmem_limit_bytes=53 << 20
        ),
    )(*(pltpu.with_memory_space_constraint(a, pltpu.HBM) for a in (tokens, grad_out, error[0], q_start.T)))
    p_factor, q_factor = pl.pallas_call(
        finish,
        out_shape=(
            jax.ShapeDtypeStruct((rank, width), F32),
            jax.ShapeDtypeStruct((rank, hidden), F32),
        ),
        in_specs=[pl.BlockSpec(memory_space=pltpu.VMEM)] * 3,
        out_specs=(pl.BlockSpec(memory_space=pl.ANY),) * 2,
        scratch_shapes=[vmem((rank, hidden), F32), dma((3,))],
        compiler_params=pltpu.CompilerParams(vmem_limit_bytes=53 << 20),
    )(p_factor, scaled, total)
    return (p_factor.T, q_factor.T)


def solution(mesh):
    in_specs = (P("dp", "tensor"), P("dp", "tensor"), P("dp", None, "tensor"), P("tensor", None))
    out_specs = (P(), P("tensor", None))
    return jax.shard_map(
        on_device, mesh=mesh, in_specs=in_specs, out_specs=out_specs, check_vma=False
    )
```
